256 devices in a mesh: dp: 64 (over x_hi, z, y), tensor: 4 (over x_lo, core).
Axes of the slice: x: 4 (x_hi: 2, x_lo: 2; x = x_hi * 2 + x_lo), y: 4, z: 8, core: 2. Of those that a mesh axis runs over, the one named last changes fastest.
Arguments:
- queries: bfloat16 [2048, 128, 576], P('dp', 'tensor')
- latent_cache: bfloat16 [2048, 128, 576], P('dp')
- lengths: int32 [2048], P('dp'), may hold values from 2 to 128, as said below
- value_up: bfloat16 [128, 512, 128], P('tensor'), may hold values from -0.25 to 0.25
- out_proj: bfloat16 [16384, 3584], P('tensor', 'dp'), may hold values from -0.046875 to 0.046875
- norm_gain: float32 [3584], replicated, may hold values from 0.25 to 1.75
- routes: int32 [2048, 8], P('dp'), may hold values from 0 to 255, all different within a row; in each aligned block of 32 rows (0 to 31, 32 to 63, ...) at most 4 rows name the same one
- route_weight: float32 [2048, 8], P('dp'), may hold values from 0.2 to 1
- expert_home: int32 [256], replicated, may hold values from -1 to 63, as said below
- w_gate: bfloat16 [64, 3584, 1024], P('dp', None, 'tensor'), may hold values from -0.09375 to 0.09375
- w_up: bfloat16 [64, 3584, 1024], P('dp', None, 'tensor'), may hold values from -0.09375 to 0.09375
- w_down: bfloat16 [64, 1024, 3584], P('dp', 'tensor'), may hold values from -0.1875 to 0.1875
Outputs:
- attended: bfloat16 [2048, 3584], P('dp')
- experts_out: bfloat16 [2048, 3584], P('dp', 'tensor')
The draws below stay inside these ranges and needn't reach their ends.
Inputs may be any that keep to these rules, and one draw needn't show every extreme that they name: `lengths`: every row has length 2 or more; some row reaches 128. `routes`: the 8 experts of a row differ; in the 32 rows of one index of dp no expert is named more than 4 times, a bound that some block reaches. `expert_home`: each of 0 to 63 is the value of exactly one expert; all other experts hold -1.
All inputs are finite; a program needn't handle non-finite values.
Results may differ from the reference program's by a relative error of at most 0.03.
Values may be sent and summed in bfloat16 or wider, within the bound.
No kernel may reach another device: no remote copies, remote signals or barrier semaphores. Data moves between devices by JAX's collectives and lax.ppermute only.
A program may use at most 128 MiB of HBM per device.

```python
import math
import jax
import jax.numpy as jnp
import numpy as np
from jax import lax

D = 3584
HEADS = 128
LATENT = 512
ROPE = 64
VDIM = 128
EXPERTS = 256
TOP = 8
FF = 1024
ROWS = 32
LMAX = 128
MOST = 4
EXP_WIN = 64
TOKENS = 2048
N_DP = 64


def shared_cache(key):
    return jax.random.normal(key, (TOKENS, LMAX, LATENT + ROPE), jnp.float32)


def draw_latent_cache(key, part):
    base = shared_cache(key)
    return base.astype(jnp.bfloat16)


def draw_queries(key, part):
    key = jax.random.fold_in(key, 12)
    noise = jax.random.normal(key, (TOKENS, HEADS, LATENT + ROPE), jnp.float32)
    return noise.astype(jnp.bfloat16)


def draw_lengths(key, part):
    key = jax.random.fold_in(key, 13)
    first_key, second_key = jax.random.split(key)
    groups = TOKENS // ROWS
    tops = jax.random.randint(first_key, (groups,), LMAX // 4, LMAX + 1)
    per_row = jnp.repeat(tops, ROWS, total_repeat_length=TOKENS)
    picked = jax.random.randint(second_key, (TOKENS,), 2, per_row + 1)
    return picked.at[0].set(LMAX).astype(jnp.int32)


def draw_expert_home(key, part):
    key = jax.random.fold_in(key, 14)
    shuffled = jax.random.permutation(key, EXPERTS)
    homes = jnp.full((EXPERTS,), -1, jnp.int32)
    return homes.at[shuffled[:EXP_WIN]].set(jnp.arange(EXP_WIN, dtype=jnp.int32))


def steps_of(rng, shape, cuts, low, high):
    loudness, own = 1.0, jax.random.fold_in(rng, 6)
    for position, shards_of in cuts:
        draws = jnp.exp(jax.random.uniform(jax.random.fold_in(own, position), (shards_of,), jnp.float32, low / len(cuts), high / len(cuts)))
        loudness = loudness * jnp.repeat(draws, shape[position] // shards_of).reshape([-1 if axis == position else 1 for axis in range(len(shape))])
    return loudness


def routed_block(rng, own, number, rows, amount, top, reach, skew):
    order = jax.random.permutation(rng, amount)
    packed, usual = shares(amount, rows * top, reach, skew, True), shares(amount, rows * top, reach, skew, False)
    places = jnp.arange(amount)

    def named(tallies, rotation):
        used = int((tallies > 0).sum())
        fixed = max(1, used // 4)
        shifted = fixed + (places - fixed + rotation * (used - fixed)) % max(1, amount - fixed)
        return jnp.zeros((amount,), jnp.int32).at[order[jnp.where(places < fixed, places, shifted)]].set(jnp.asarray(tallies, jnp.int32))

    tallies = jnp.where(number % 4 == 0, named(packed, number // 4), named(usual, number - number // 4 - 1))
    mixed = jax.random.permutation(jax.random.fold_in(own, 3), amount)
    giver, taker = mixed[0:amount // 2 * 2:2], mixed[1:amount // 2 * 2:2]
    margin = jnp.minimum(tallies[giver] - 1, reach - tallies[taker]) // 2
    margin = jnp.where((giver == order[0]) | (taker == order[0]) | (tallies[taker] == 0), 0, jnp.maximum(margin, 0))
    shifted = jax.random.randint(jax.random.fold_in(own, 4), (amount // 2,), 0, 1 << 20) % (margin + 1)
    tallies = tallies.at[giver].add(-shifted).at[taker].add(shifted)
    labels = jnp.searchsorted(jnp.cumsum(tallies), jnp.arange(rows * top), side="right").astype(jnp.int32)
    table = labels.reshape(top, rows).T
    table = table[jax.random.permutation(jax.random.fold_in(own, 1), rows)]
    rotation = jax.random.randint(jax.random.fold_in(own, 2), (rows, 1), 0, top)
    return jnp.take_along_axis(table, (jnp.arange(top)[None, :] + rotation) % top, axis=1)


def shares(number_of, total, reach, lean, full):
    weights = [(1 << 20) // math.isqrt(rank ** lean) + 1 for rank in range(1, number_of + 1)]
    largest = reach if full else min(reach, max(-(-total // number_of), total * weights[0] // sum(weights)))
    least = 1 if total - largest >= number_of - 1 else 0
    given, surplus = [largest] + [least] * (number_of - 1), total - largest - least * (number_of - 1)
    while surplus > 0:
        movable = [i for i in range(1, number_of) if given[i] < largest] or [i for i in range(1, number_of) if given[i] < reach]
        whole, left = sum([weights[i] for i in movable]), surplus
        for i in movable:
            more = min(reach - given[i], max(1, left * weights[i] // whole), surplus)
            given[i] = given[i] + more
            surplus = surplus - more
    return np.array(given)


def bell_draw(rng, dims, deviation, limit, shards=(), held_as=jnp.bfloat16):
    entries = jax.random.normal(rng, dims, jnp.float32) * deviation
    if len(shards) > 0:
        entries = steps_of(rng, dims, shards, -0.22, 0.18) * entries
    return jnp.clip(entries, min=-limit, max=limit).astype(held_as)


def setup_inputs(seed: int = 0) -> dict:
    key_of = jax.random.split(jax.random.key(seed), 13)
    queries = draw_queries(jax.random.fold_in(key_of[12], 71), 0)
    latent_cache = draw_latent_cache(jax.random.fold_in(key_of[12], 71), 0)
    lengths = draw_lengths(jax.random.fold_in(key_of[12], 71), 0)
    value_up = bell_draw(key_of[3], (HEADS, LATENT, VDIM), LATENT ** -0.5, 0.25, ((0, 4),))
    out_proj = bell_draw(key_of[4], (HEADS * VDIM, D), (HEADS * VDIM) ** -0.5, 0.046875, ((0, 4), (1, 64)))
    norm_gain = jnp.clip(1.0 + 0.15 * jax.random.normal(key_of[5], (D,), jnp.float32), 0.25, 1.75)
    routes_keys = jax.random.split(jax.random.fold_in(key_of[6], 1), TOKENS // ROWS)
    routes_turns = jax.random.permutation(jax.random.fold_in(key_of[6], 3), TOKENS // ROWS)
    routes = jax.vmap(lambda own, number: routed_block(jax.random.fold_in(key_of[6], 2), own, number, ROWS, EXPERTS, TOP, MOST, 2))(routes_keys, routes_turns).reshape((TOKENS, TOP))
    route_weight = jnp.clip(0.2 + 0.8 * jax.random.uniform(key_of[7], (TOKENS, TOP), jnp.float32) ** steps_of(key_of[7], (TOKENS, TOP), ((0, 64),), -0.2, 0.2), 0.2, 1.0)
    expert_home = draw_expert_home(jax.random.fold_in(key_of[12], 71), 0)
    w_gate = bell_draw(key_of[9], (EXP_WIN, D, FF), D ** -0.5, 0.09375, ((0, 64), (2, 4)))
    w_up = bell_draw(key_of[10], (EXP_WIN, D, FF), D ** -0.5, 0.09375, ((0, 64), (2, 4)))
    w_down = bell_draw(key_of[11], (EXP_WIN, FF, D), FF ** -0.5, 0.1875, ((0, 64), (1, 4)))
    return {"queries": queries, "latent_cache": latent_cache, "lengths": lengths, "value_up": value_up, "out_proj": out_proj, "norm_gain": norm_gain, "routes": routes, "route_weight": route_weight, "expert_home": expert_home, "w_gate": w_gate, "w_up": w_up, "w_down": w_down}


softmax_scale = 192.0 ** (-0.5)
norm_eps = 1e-06

def rounded(value):
    return lax.optimization_barrier(value.astype(jnp.bfloat16))

def reference(queries, latent_cache, lengths, value_up, out_proj, norm_gain, routes, route_weight, expert_home, w_gate, w_up, w_down):
    query_f = queries.astype(jnp.float32)
    cache_f = latent_cache.astype(jnp.float32)
    scores = jnp.einsum('thc,tjc->thj', query_f, cache_f) * softmax_scale
    visible = jnp.arange(LMAX, dtype=jnp.int32)[None, None, :] < lengths[:, None, None]
    scores = jnp.where(visible, scores, -jnp.inf)
    row_max = lax.optimization_barrier(jnp.max(scores, axis=2, keepdims=True))
    exponent = jnp.exp(scores - row_max)
    weights = rounded(exponent / lax.optimization_barrier(jnp.sum(exponent, axis=2, keepdims=True)))
    latent_out = rounded(jnp.einsum('thj,tjc->thc', weights.astype(jnp.float32), cache_f[:, :, :LATENT]))
    values = rounded(jnp.einsum('thc,hcv->thv', latent_out.astype(jnp.float32), value_up.astype(jnp.float32)))
    attended = jnp.dot(values.reshape(TOKENS, HEADS * VDIM), out_proj, preferred_element_type=jnp.float32).astype(jnp.bfloat16)
    attended_f = attended.astype(jnp.float32)
    mean_square = lax.optimization_barrier(jnp.mean(attended_f * attended_f, axis=1, keepdims=True))
    normed = (attended_f * lax.rsqrt(mean_square + norm_eps) * norm_gain).astype(jnp.bfloat16)
    home_of = expert_home[routes]
    capacity = N_DP * MOST

    def one_expert(accum, carried):
        expert_slot, gate_weight, up_weight, down_weight = carried
        routed = home_of == expert_slot
        chosen = jnp.any(routed, axis=1)
        scale_of = lax.optimization_barrier(jnp.sum(jnp.where(routed, route_weight, jnp.zeros_like(route_weight)), axis=1))
        picked = jnp.nonzero(chosen, size=capacity, fill_value=0)[0].astype(jnp.int32)
        filled = jnp.arange(capacity, dtype=jnp.int32) < jnp.sum(chosen.astype(jnp.int32))
        picked_rows = normed[picked]
        gate_out = jnp.dot(picked_rows, gate_weight, preferred_element_type=jnp.float32)
        up_out = jnp.dot(picked_rows, up_weight, preferred_element_type=jnp.float32)
        hidden = (jax.nn.silu(gate_out) * up_out).astype(jnp.bfloat16)
        result = rounded(jnp.dot(hidden, down_weight, preferred_element_type=jnp.float32)).astype(jnp.float32)
        factor = jnp.where(filled, scale_of[picked], jnp.zeros_like(scale_of[picked]))
        return (accum.at[picked].add(factor[:, None] * result), None)
    start = jnp.zeros((TOKENS, D), jnp.float32)
    accum, unused = lax.scan(one_expert, start, (jnp.arange(EXP_WIN, dtype=jnp.int32), w_gate, w_up, w_down))
    return (attended, accum.astype(jnp.bfloat16))
```

```python
import jax
import jax.numpy as jnp
from jax import lax
from jax.sharding import Mesh, PartitionSpec as P

LATENT = 512
MOST = 4

softmax_scale = 192.0 ** (-0.5)
norm_eps = 1e-06

AXES = ("xh", "z", "y", "xl", "core")
DP = ("xh", "z", "y")
TENSOR = ("xl", "core")
bf16 = jnp.bfloat16
f32 = jnp.float32


def flip(value, axis, mask=1):
    count = lax.axis_size(axis)
    return lax.ppermute(value, axis, [(i, i ^ mask) for i in range(count)])


def exchange(value, axis):
    return lax.all_to_all(value, axis, split_axis=0, concat_axis=0, tiled=True)


def dot_t(left, right):
    return lax.dot_general(left, right, (((1,), (1,)), ((), ())), preferred_element_type=f32)


def pair(where_zero, mine, other):
    return jnp.where(where_zero, mine, other), jnp.where(where_zero, other, mine)


def attention(queries, latent_cache, lengths, value_up):
    scores = (
        jnp.einsum("rhc,rjc->rhj", queries, latent_cache, preferred_element_type=f32)
        * softmax_scale
    )
    visible = (
        lax.broadcasted_iota(jnp.int32, (1, 1, latent_cache.shape[1]), 2) < lengths[:, None, None]
    )
    scores = jnp.where(visible, scores, -jnp.inf)
    row_max = jnp.max(scores, axis=2, keepdims=True)
    exponent = jnp.exp(scores - row_max)
    weights = (exponent / jnp.sum(exponent, axis=2, keepdims=True)).astype(bf16)
    latent_out = jnp.einsum(
        "rhj,rjc->rhc", weights, latent_cache[:, :, :LATENT], preferred_element_type=f32
    ).astype(bf16)
    values = jnp.einsum("rhc,hcv->rhv", latent_out, value_up, preferred_element_type=f32)
    return values.astype(bf16).reshape(queries.shape[0], -1)


def placing(routes, expert_home, owners):
    catalog = jnp.arange(expert_home.shape[0], dtype=jnp.int32)
    matches = routes[:, :, None] == catalog[None, None, :]
    home_of = jnp.sum(jnp.where(matches, expert_home[None, None, :], 0), axis=2)
    owner_ids = jnp.arange(owners, dtype=jnp.int32)
    on_owner = home_of[:, :, None] == owner_ids[None, None, :]
    chosen = jnp.any(on_owner, axis=1)
    order_in = jnp.cumsum(chosen.astype(jnp.int32), axis=0) - 1
    slot_ids = jnp.arange(MOST, dtype=jnp.int32)
    slot_map = chosen[:, :, None] & (order_in[:, :, None] == slot_ids[None, None, :])
    return on_owner, slot_map


def shards(
    queries,
    latent_cache,
    lengths,
    value_up,
    out_proj,
    norm_gain,
    routes,
    route_weight,
    expert_home,
    w_gate,
    w_up,
    w_down,
):
    rows_here = queries.shape[0]
    xh, y, xl, core = (lax.axis_index(name) for name in ("xh", "y", "xl", "core"))
    n_z, n_y = lax.axis_size("z"), lax.axis_size("y")
    owners = lax.axis_size(DP)
    tensor_at = lax.axis_index(TENSOR)
    n_tensor = lax.axis_size(TENSOR)
    width = norm_gain.shape[0]
    quarter = width // n_tensor

    cols = out_proj.shape[1]
    depth = out_proj.shape[0] // n_z
    proj = out_proj.T.reshape(cols, n_z, depth).transpose(1, 0, 2)
    proj = exchange(proj, "z")
    half = n_z // 2
    proj_mine = lax.dynamic_slice_in_dim(proj, xl * half, half, 0)
    proj_other = flip(lax.dynamic_slice_in_dim(proj, (1 - xl) * half, half, 0), "xl")
    proj_both = jnp.stack([proj_mine, proj_other])
    over_y = jnp.stack([proj_both] + [flip(proj_both, "y", s) for s in range(1, n_y)])
    over_y = jnp.stack(
        [lax.dynamic_index_in_dim(over_y, y ^ s, 0, keepdims=False) for s in range(n_y)], axis=2
    )
    proj_own = over_y[0].reshape(quarter, depth)
    proj_oth = over_y[1].reshape(quarter, depth)

    down = []
    for s in range(n_tensor):
        piece = lax.dynamic_slice_in_dim(w_down[0], (tensor_at ^ s) * quarter, quarter, 1)
        down.append(flip(piece, TENSOR, s) if s else piece)

    swap = [(i, (i % 2) * 2 + i // 2) for i in range(4)]
    routes_sent = lax.ppermute(routes, ("xh", "core"), swap)

    values = attention(queries, latent_cache, lengths, value_up)
    values = values.reshape(rows_here, n_z, depth).transpose(1, 0, 2)
    values = exchange(values, "z").reshape(n_z * rows_here, depth)
    from_xl = flip(values, "xl")
    from_xh = flip(values, "xh")
    from_both = flip(values, ("xh", "xl"), 3)
    here = xh == core
    keep_own, send_own = pair(here, values, from_xh)
    keep_oth, send_oth = pair(here, from_xl, from_both)
    partial_send = (dot_t(send_own, proj_own) + dot_t(send_oth, proj_oth)).astype(bf16)
    partial_got = flip(partial_send, "core")
    partial = dot_t(keep_own, proj_own) + dot_t(keep_oth, proj_oth) + partial_got.astype(f32)
    partial = partial.astype(bf16).reshape(n_z, rows_here, quarter)
    partial = exchange(partial, "z")
    part_rows = jnp.sum(partial.astype(f32), axis=0).astype(bf16)

    _, slots_sent = placing(routes_sent, expert_home, owners)
    outgoing = jnp.einsum(
        "roc,rd->ocd", slots_sent.astype(bf16), part_rows, preferred_element_type=f32
    ).astype(bf16)
    incoming = exchange(outgoing, DP).reshape(2, -1, quarter)

    in_xl = flip(incoming, "xl")
    in_core = flip(incoming, "core")
    in_both = flip(in_xl, "core")
    own_xl = jnp.concatenate(pair(core == 0, incoming, in_core), axis=1)
    oth_xl = jnp.concatenate(pair(core == 0, in_xl, in_both), axis=1)
    xl_zero, xl_one = pair(xl == 0, own_xl, oth_xl)
    stacked = [xl_zero[0], xl_one[0], xl_zero[1], xl_one[1]]
    stacked_f = [piece.astype(f32) for piece in stacked]
    mean_square = sum(jnp.sum(p * p, axis=1, keepdims=True) for p in stacked_f) / width
    scale = lax.rsqrt(mean_square + norm_eps)
    gate_out, up_out = 0.0, 0.0
    for q in range(n_tensor):
        span = slice(q * quarter, (q + 1) * quarter)
        normed = (stacked_f[q] * scale * norm_gain[span]).astype(bf16)
        gate_out += jnp.dot(normed, w_gate[0, span], preferred_element_type=f32)
        up_out += jnp.dot(normed, w_up[0, span], preferred_element_type=f32)
    hidden = (jax.nn.silu(gate_out) * up_out).astype(bf16)
    hid_xl = flip(hidden, "xl")
    hid_core = flip(hidden, "core")
    hid_both = flip(hid_xl, "core")
    result = 0.0
    for piece, weight in zip((hidden, hid_core, hid_xl, hid_both), down):
        result += jnp.dot(piece, weight, preferred_element_type=f32)
    returned = exchange(result.astype(bf16).reshape(owners, MOST, quarter), DP)

    on_owner, slot_map = placing(routes, expert_home, owners)
    share_weight = jnp.sum(jnp.where(on_owner, route_weight[:, :, None], 0.0), axis=1)
    combine_weight = slot_map.astype(f32) * share_weight[:, :, None]
    experts_out = jnp.einsum("roc,ocd->rd", combine_weight, returned.astype(f32)).astype(bf16)

    row_xl = flip(part_rows, "xl")
    lower, upper = pair(xl == 0, part_rows, row_xl)
    mine = jnp.concatenate([lower, upper], axis=1)
    row_xh = flip(mine, "xh")
    lower, upper = pair(xh == 0, mine, row_xh)
    whole = jnp.concatenate([lower, upper], axis=1)
    attended = jnp.where(here, whole, flip(whole, "core"))
    return (attended, experts_out)


def solution(mesh):
    fine = Mesh(mesh.devices.reshape(2, 8, 4, 2, 2), AXES)
    return jax.shard_map(
        shards,
        mesh=fine,
        in_specs=(
            P(DP, TENSOR, None),
            P(DP, None, None),
            P(DP),
            P(TENSOR, None, None),
            P(TENSOR, DP),
            P(),
            P(DP, None),
            P(DP, None),
            P(),
            P(DP, None, TENSOR),
            P(DP, None, TENSOR),
            P(DP, TENSOR, None),
        ),
        out_specs=(P(DP, None), P(DP, TENSOR)),
        check_vma=False,
    )
```

```python
import jax
import jax.numpy as jnp
from jax import lax
from jax.sharding import Mesh, PartitionSpec as P

LATENT = 512
MOST = 4

softmax_scale = 192.0 ** (-0.5)
norm_eps = 1e-06

AXES = ("xh", "z", "y", "xl", "core")
DP = ("xh", "z", "y")
TENSOR = ("xl", "core")
bf16 = jnp.bfloat16
f32 = jnp.float32


def flip(value, axis, mask=1):
    count = lax.axis_size(axis)
    return lax.ppermute(value, axis, [(i, i ^ mask) for i in range(count)])


def exchange(value, axis):
    return lax.all_to_all(value, axis, split_axis=0, concat_axis=0, tiled=True)


def dot_t(left, right):
    return lax.dot_general(left, right, (((1,), (1,)), ((), ())), preferred_element_type=f32)


def pair(where_zero, mine, other):
    return jnp.where(where_zero, mine, other), jnp.where(where_zero, other, mine)


def attention(queries, latent_cache, lengths, value_up):
    scores = (
        jnp.einsum("rhc,rjc->rhj", queries, latent_cache, preferred_element_type=f32)
        * softmax_scale
    )
    visible = (
        lax.broadcasted_iota(jnp.int32, (1, 1, latent_cache.shape[1]), 2) < lengths[:, None, None]
    )
    scores = jnp.where(visible, scores, -jnp.inf)
    row_max = jnp.max(scores, axis=2, keepdims=True)
    exponent = jnp.exp(scores - row_max)
    weights = (exponent / jnp.sum(exponent, axis=2, keepdims=True)).astype(bf16)
    latent_out = jnp.einsum(
        "rhj,rjc->rhc", weights, latent_cache[:, :, :LATENT], preferred_element_type=f32
    ).astype(bf16)
    values = jnp.einsum("rhc,hcv->rhv", latent_out, value_up, preferred_element_type=f32)
    return values.astype(bf16).reshape(queries.shape[0], -1)


def placing(routes, expert_home, owners):
    catalog = jnp.arange(expert_home.shape[0], dtype=jnp.int32)
    matches = routes[:, :, None] == catalog[None, None, :]
    home_of = jnp.sum(jnp.where(matches, expert_home[None, None, :], 0), axis=2)
    owner_ids = jnp.arange(owners, dtype=jnp.int32)
    on_owner = home_of[:, :, None] == owner_ids[None, None, :]
    chosen = jnp.any(on_owner, axis=1)
    order_in = jnp.cumsum(chosen.astype(jnp.int32), axis=0) - 1
    slot_ids = jnp.arange(MOST, dtype=jnp.int32)
    slot_map = chosen[:, :, None] & (order_in[:, :, None] == slot_ids[None, None, :])
    return on_owner, slot_map


def shards(
    queries,
    latent_cache,
    lengths,
    value_up,
    out_proj,
    norm_gain,
    routes,
    route_weight,
    expert_home,
    w_gate,
    w_up,
    w_down,
):
    rows_here = queries.shape[0]
    xh, y, xl, core = (lax.axis_index(name) for name in ("xh", "y", "xl", "core"))
    n_z, n_y = lax.axis_size("z"), lax.axis_size("y")
    owners = lax.axis_size(DP)
    tensor_at = lax.axis_index(TENSOR)
    n_tensor = lax.axis_size(TENSOR)
    width = norm_gain.shape[0]
    quarter = width // n_tensor

    cols = out_proj.shape[1]
    depth = out_proj.shape[0] // n_z
    proj = out_proj.T.reshape(cols, n_z, depth).transpose(1, 0, 2)
    proj = exchange(proj, "z")
    values = attention(queries, latent_cache, lengths, value_up)
    proj, values = lax.optimization_barrier((proj, values))
    half = n_z // 2
    proj_leaving = lax.dynamic_slice_in_dim(proj, (1 - xl) * half, half, 0)
    proj_other = flip(proj_leaving, "xl")
    proj_mine = lax.dynamic_slice_in_dim(proj, xl * half, half, 0)
    over_y = jnp.concatenate([proj_mine, proj_other], axis=0)
    over_y = jnp.stack([over_y] + [flip(over_y, "y", s) for s in range(1, n_y)])
    over_y = over_y.reshape(n_y, 2, half, cols, depth)
    over_y = jnp.stack(
        [lax.dynamic_index_in_dim(over_y, y ^ s, 0, keepdims=False) for s in range(n_y)], axis=2
    )
    proj_own = over_y[0].reshape(quarter, depth)
    proj_oth = over_y[1].reshape(quarter, depth)

    down = []
    for s in range(n_tensor):
        piece = lax.dynamic_slice_in_dim(w_down[0], (tensor_at ^ s) * quarter, quarter, 1)
        down.append(flip(piece, TENSOR, s) if s else piece)

    swap = [(i, (i % 2) * 2 + i // 2) for i in range(4)]
    routes_sent = lax.ppermute(routes, ("xh", "core"), swap)

    values = values.reshape(rows_here, n_z, depth).transpose(1, 0, 2)
    values = exchange(values, "z").reshape(n_z * rows_here, depth)
    from_xl = flip(values, "xl")
    from_xh = flip(values, "xh")
    from_both = flip(values, ("xh", "xl"), 3)
    here = xh == core
    keep_own, send_own = pair(here, values, from_xh)
    keep_oth, send_oth = pair(here, from_xl, from_both)
    partial_send = (dot_t(send_own, proj_own) + dot_t(send_oth, proj_oth)).astype(bf16)
    partial_got = flip(partial_send, "core")
    partial = dot_t(keep_own, proj_own) + dot_t(keep_oth, proj_oth) + partial_got.astype(f32)
    partial = partial.astype(bf16).reshape(n_z, rows_here, quarter)
    partial = exchange(partial, "z")
    part_rows = jnp.sum(partial.astype(f32), axis=0).astype(bf16)

    _, slots_sent = placing(routes_sent, expert_home, owners)
    outgoing = jnp.einsum(
        "roc,rd->ocd", slots_sent.astype(bf16), part_rows, preferred_element_type=f32
    ).astype(bf16)
    incoming = exchange(outgoing, DP).reshape(2, -1, quarter)

    in_xl = flip(incoming, "xl")
    in_core = flip(incoming, "core")
    in_both = flip(in_xl, "core")
    own_xl = jnp.concatenate(pair(core == 0, incoming, in_core), axis=1)
    oth_xl = jnp.concatenate(pair(core == 0, in_xl, in_both), axis=1)
    xl_zero, xl_one = pair(xl == 0, own_xl, oth_xl)
    stacked = [xl_zero[0], xl_one[0], xl_zero[1], xl_one[1]]
    stacked_f = [piece.astype(f32) for piece in stacked]
    mean_square = sum(jnp.sum(p * p, axis=1, keepdims=True) for p in stacked_f) / width
    scale = lax.rsqrt(mean_square + norm_eps)
    gate_out, up_out = 0.0, 0.0
    for q in range(n_tensor):
        span = slice(q * quarter, (q + 1) * quarter)
        normed = (stacked_f[q] * scale * norm_gain[span]).astype(bf16)
        gate_out += jnp.dot(normed, w_gate[0, span], preferred_element_type=f32)
        up_out += jnp.dot(normed, w_up[0, span], preferred_element_type=f32)
    hidden = (jax.nn.silu(gate_out) * up_out).astype(bf16)
    hid_xl = flip(hidden, "xl")
    hid_core = flip(hidden, "core")
    hid_both = flip(hid_xl, "core")
    result = 0.0
    for piece, weight in zip((hidden, hid_core, hid_xl, hid_both), down):
        result += jnp.dot(piece, weight, preferred_element_type=f32)
    returned = exchange(result.astype(bf16).reshape(owners, MOST, quarter), DP)

    on_owner, slot_map = placing(routes, expert_home, owners)
    share_weight = jnp.sum(jnp.where(on_owner, route_weight[:, :, None], 0.0), axis=1)
    combine_weight = slot_map.astype(f32) * share_weight[:, :, None]
    experts_out = jnp.einsum("roc,ocd->rd", combine_weight, returned.astype(f32)).astype(bf16)

    row_xl = flip(part_rows, "xl")
    lower, upper = pair(xl == 0, part_rows, row_xl)
    mine = jnp.concatenate([lower, upper], axis=1)
    row_xh = flip(mine, "xh")
    lower, upper = pair(xh == 0, mine, row_xh)
    whole = jnp.concatenate([lower, upper], axis=1)
    attended = jnp.where(here, whole, flip(whole, "core"))
    return (attended, experts_out)


def solution(mesh):
    fine = Mesh(mesh.devices.reshape(2, 8, 4, 2, 2), AXES)
    return jax.shard_map(
        shards,
        mesh=fine,
        in_specs=(
            P(DP, TENSOR, None),
            P(DP, None, None),
            P(DP),
            P(TENSOR, None, None),
            P(TENSOR, DP),
            P(),
            P(DP, None),
            P(DP, None),
            P(),
            P(DP, None, TENSOR),
            P(DP, None, TENSOR),
            P(DP, TENSOR, None),
        ),
        out_specs=(P(DP, None), P(DP, TENSOR)),
        check_vma=False,
    )
```

```python
import jax
import jax.numpy as jnp
from jax import lax
from jax.sharding import Mesh, PartitionSpec as P

LATENT = 512
MOST = 4

softmax_scale = 192.0 ** (-0.5)
norm_eps = 1e-06

AXES = ("xh", "z", "y", "xl", "core")
DP = ("xh", "z", "y")
TENSOR = ("xl", "core")
bf16 = jnp.bfloat16
f32 = jnp.float32


def flip(value, axis, mask=1):
    count = lax.axis_size(axis)
    return lax.ppermute(value, axis, [(i, i ^ mask) for i in range(count)])


def exchange(value, axis):
    return lax.all_to_all(value, axis, split_axis=0, concat_axis=0, tiled=True)


def dot_t(left, right):
    return lax.dot_general(left, right, (((1,), (1,)), ((), ())), preferred_element_type=f32)


def pair(where_zero, mine, other):
    return jnp.where(where_zero, mine, other), jnp.where(where_zero, other, mine)


def attention(queries, latent_cache, lengths, value_up):
    scores = (
        jnp.einsum("rhc,rjc->rhj", queries, latent_cache, preferred_element_type=f32)
        * softmax_scale
    )
    visible = (
        lax.broadcasted_iota(jnp.int32, (1, 1, latent_cache.shape[1]), 2) < lengths[:, None, None]
    )
    scores = jnp.where(visible, scores, -jnp.inf)
    row_max = jnp.max(scores, axis=2, keepdims=True)
    exponent = jnp.exp(scores - row_max)
    weights = (exponent / jnp.sum(exponent, axis=2, keepdims=True)).astype(bf16)
    latent_out = jnp.einsum(
        "rhj,rjc->rhc", weights, latent_cache[:, :, :LATENT], preferred_element_type=f32
    ).astype(bf16)
    values = jnp.einsum("rhc,hcv->rhv", latent_out, value_up, preferred_element_type=f32)
    return values.astype(bf16).reshape(queries.shape[0], -1)


def placing(routes, expert_home, owners):
    catalog = jnp.arange(expert_home.shape[0], dtype=jnp.int32)
    matches = routes[:, :, None] == catalog[None, None, :]
    home_of = jnp.sum(jnp.where(matches, expert_home[None, None, :], 0), axis=2)
    owner_ids = jnp.arange(owners, dtype=jnp.int32)
    on_owner = home_of[:, :, None] == owner_ids[None, None, :]
    chosen = jnp.any(on_owner, axis=1)
    order_in = jnp.cumsum(chosen.astype(jnp.int32), axis=0) - 1
    slot_ids = jnp.arange(MOST, dtype=jnp.int32)
    slot_map = chosen[:, :, None] & (order_in[:, :, None] == slot_ids[None, None, :])
    return on_owner, slot_map


def shards(
    queries,
    latent_cache,
    lengths,
    value_up,
    out_proj,
    norm_gain,
    routes,
    route_weight,
    expert_home,
    w_gate,
    w_up,
    w_down,
):
    rows_here = queries.shape[0]
    xh, y, xl, core = (lax.axis_index(name) for name in ("xh", "y", "xl", "core"))
    n_z, n_y = lax.axis_size("z"), lax.axis_size("y")
    owners = lax.axis_size(DP)
    tensor_at = lax.axis_index(TENSOR)
    n_tensor = lax.axis_size(TENSOR)
    width = norm_gain.shape[0]
    quarter = width // n_tensor

    cols = out_proj.shape[1]
    depth = out_proj.shape[0] // n_z
    proj = out_proj.T.reshape(cols, n_z, depth).transpose(1, 0, 2)
    proj = exchange(proj, "z")
    values = attention(queries, latent_cache, lengths, value_up)
    proj, values = lax.optimization_barrier((proj, values))
    half = n_z // 2
    proj_leaving = lax.dynamic_slice_in_dim(proj, (1 - xl) * half, half, 0)
    proj_other = flip(proj_leaving, "xl")
    proj_mine = lax.dynamic_slice_in_dim(proj, xl * half, half, 0)
    over_y = jnp.concatenate([proj_mine, proj_other], axis=0)
    over_y = [over_y] + [flip(over_y, "y", s) for s in range(1, n_y)]
    values = values.reshape(rows_here, n_z, depth).transpose(1, 0, 2)
    values = exchange(values, "z").reshape(n_z * rows_here, depth)
    from_xh = flip(values, "xh")
    from_both = flip(values, ("xh", "xl"), 3)
    over_y[1], values_late = lax.optimization_barrier((over_y[1], values))
    from_xl = flip(values_late, "xl")
    over_y = jnp.stack(over_y)
    over_y = over_y.reshape(n_y, 2, half, cols, depth)
    over_y = jnp.stack(
        [lax.dynamic_index_in_dim(over_y, y ^ s, 0, keepdims=False) for s in range(n_y)], axis=2
    )
    proj_own = over_y[0].reshape(quarter, depth)
    proj_oth = over_y[1].reshape(quarter, depth)

    here = xh == core
    keep_own, send_own = pair(here, values, from_xh)
    keep_oth, send_oth = pair(here, from_xl, from_both)
    partial_send = (dot_t(send_own, proj_own) + dot_t(send_oth, proj_oth)).astype(bf16)
    partial_got = flip(partial_send, "core")
    partial = dot_t(keep_own, proj_own) + dot_t(keep_oth, proj_oth) + partial_got.astype(f32)
    partial = partial.astype(bf16).reshape(n_z, rows_here, quarter)
    w_down, partial, routes_late = lax.optimization_barrier((w_down, partial, routes))
    partial = exchange(partial, "z")
    swap = [(i, (i % 2) * 2 + i // 2) for i in range(4)]
    routes_sent = lax.ppermute(routes_late, ("xh", "core"), swap)

    down = []
    for s in range(n_tensor):
        piece = lax.dynamic_slice_in_dim(w_down[0], (tensor_at ^ s) * quarter, quarter, 1)
        down.append(flip(piece, TENSOR, s) if s else piece)

    part_rows = jnp.sum(partial.astype(f32), axis=0).astype(bf16)

    _, slots_sent = placing(routes_sent, expert_home, owners)
    outgoing = jnp.einsum(
        "roc,rd->ocd", slots_sent.astype(bf16), part_rows, preferred_element_type=f32
    ).astype(bf16)
    outgoing, w_gate, w_up = lax.optimization_barrier((outgoing, w_gate, w_up))
    incoming = exchange(outgoing, DP).reshape(2, -1, quarter)

    def folded(weight, side):
        weight = weight.reshape(2, 2, quarter, -1)
        gains = norm_gain.reshape(2, 2, quarter, 1)
        weight = lax.dynamic_index_in_dim(weight, side, 1, keepdims=False)
        gains = lax.dynamic_index_in_dim(gains, side, 1, keepdims=False)
        return (weight.astype(f32) * gains).astype(bf16)

    halves = [[folded(w, side) for w in (w_gate, w_up)] for side in (xl, 1 - xl)]
    halves, incoming = lax.optimization_barrier((halves, incoming))
    in_xl = flip(incoming, "xl")
    in_core = flip(incoming, "core")
    in_both = flip(in_xl, "core")

    def from_half(pieces, weights):
        squares, gate_out, up_out = 0.0, 0.0, 0.0
        for i in (0, 1):
            rows = pieces[i].astype(f32)
            squares += jnp.sum(rows * rows, axis=1, keepdims=True)
            gate_out += jnp.dot(pieces[i], weights[0][i], preferred_element_type=f32)
            up_out += jnp.dot(pieces[i], weights[1][i], preferred_element_type=f32)
        return squares, gate_out, up_out

    def hidden_of(own_half, other_half):
        squares, gate_out, up_out = (
            one + two
            for one, two in zip(from_half(own_half, halves[0]), from_half(other_half, halves[1]))
        )
        scale = lax.rsqrt(squares / width + norm_eps)
        return (jax.nn.silu(gate_out * scale) * (up_out * scale)).astype(bf16)

    hidden = jnp.concatenate(
        pair(core == 0, hidden_of(incoming, in_xl), hidden_of(in_core, in_both)), axis=0
    )
    hid_xl = flip(hidden, "xl")
    hid_core = flip(hidden, "core")
    result = jnp.dot(hidden, down[0], preferred_element_type=f32)
    result += jnp.dot(hid_core, down[1], preferred_element_type=f32)
    result, hid_xl = lax.optimization_barrier((result, hid_xl))
    hid_both = flip(hid_xl, "core")
    result += jnp.dot(hid_xl, down[2], preferred_element_type=f32)
    result += jnp.dot(hid_both, down[3], preferred_element_type=f32)
    row_xl = flip(part_rows, "xl")
    lower, upper = pair(xl == 0, part_rows, row_xl)
    mine = jnp.concatenate([lower, upper], axis=1)
    row_xh = flip(mine, "xh")
    lower, upper = pair(xh == 0, mine, row_xh)
    whole = jnp.concatenate([lower, upper], axis=1)
    whole, result = lax.optimization_barrier((whole, result))
    returned = exchange(result.astype(bf16).reshape(owners, MOST, quarter), DP)

    on_owner, slot_map = placing(routes, expert_home, owners)
    share_weight = jnp.sum(jnp.where(on_owner, route_weight[:, :, None], 0.0), axis=1)
    combine_weight = slot_map.astype(f32) * share_weight[:, :, None]
    experts_out = jnp.einsum("roc,ocd->rd", combine_weight, returned.astype(f32)).astype(bf16)

    attended = jnp.where(here, whole, flip(whole, "core"))
    return (attended, experts_out)


def solution(mesh):
    fine = Mesh(mesh.devices.reshape(2, 8, 4, 2, 2), AXES)
    return jax.shard_map(
        shards,
        mesh=fine,
        in_specs=(
            P(DP, TENSOR, None),
            P(DP, None, None),
            P(DP),
            P(TENSOR, None, None),
            P(TENSOR, DP),
            P(),
            P(DP, None),
            P(DP, None),
            P(),
            P(DP, None, TENSOR),
            P(DP, None, TENSOR),
            P(DP, TENSOR, None),
        ),
        out_specs=(P(DP, None), P(DP, TENSOR)),
        check_vma=False,
    )
```

```python
import jax
import jax.numpy as jnp
from jax import lax
from jax.sharding import Mesh, PartitionSpec as P

LATENT = 512
MOST = 4

softmax_scale = 192.0 ** (-0.5)
norm_eps = 1e-06

AXES = ("xh", "z", "y", "xl", "core")
DP = ("xh", "z", "y")
TENSOR = ("xl", "core")
bf16 = jnp.bfloat16
f32 = jnp.float32


def flip(value, axis, mask=1):
    count = lax.axis_size(axis)
    return lax.ppermute(value, axis, [(i, i ^ mask) for i in range(count)])


def exchange(value, axis):
    return lax.all_to_all(value, axis, split_axis=0, concat_axis=0, tiled=True)


def dot_t(left, right):
    return lax.dot_general(left, right, (((1,), (1,)), ((), ())), preferred_element_type=f32)


def pair(where_zero, mine, other):
    return jnp.where(where_zero, mine, other), jnp.where(where_zero, other, mine)


def attention(queries, latent_cache, lengths, value_up):
    scores = (
        jnp.einsum("rhc,rjc->rhj", queries, latent_cache, preferred_element_type=f32)
        * softmax_scale
    )
    visible = (
        lax.broadcasted_iota(jnp.int32, (1, 1, latent_cache.shape[1]), 2) < lengths[:, None, None]
    )
    scores = jnp.where(visible, scores, -jnp.inf)
    row_max = jnp.max(scores, axis=2, keepdims=True)
    exponent = jnp.exp(scores - row_max)
    weights = (exponent / jnp.sum(exponent, axis=2, keepdims=True)).astype(bf16)
    latent_out = jnp.einsum(
        "rhj,rjc->rhc", weights, latent_cache[:, :, :LATENT], preferred_element_type=f32
    ).astype(bf16)
    values = jnp.einsum("rhc,hcv->rhv", latent_out, value_up, preferred_element_type=f32)
    return values.astype(bf16).reshape(queries.shape[0], -1)


def placing(routes, expert_home, owners):
    catalog = jnp.arange(expert_home.shape[0], dtype=jnp.int32)
    matches = routes[:, :, None] == catalog[None, None, :]
    home_of = jnp.sum(jnp.where(matches, expert_home[None, None, :], 0), axis=2)
    owner_ids = jnp.arange(owners, dtype=jnp.int32)
    on_owner = home_of[:, :, None] == owner_ids[None, None, :]
    chosen = jnp.any(on_owner, axis=1)
    order_in = jnp.cumsum(chosen.astype(jnp.int32), axis=0) - 1
    slot_ids = jnp.arange(MOST, dtype=jnp.int32)
    slot_map = chosen[:, :, None] & (order_in[:, :, None] == slot_ids[None, None, :])
    return on_owner, slot_map


def shards(
    queries,
    latent_cache,
    lengths,
    value_up,
    out_proj,
    norm_gain,
    routes,
    route_weight,
    expert_home,
    w_gate,
    w_up,
    w_down,
):
    rows_here = queries.shape[0]
    xh, y, xl, core = (lax.axis_index(name) for name in ("xh", "y", "xl", "core"))
    n_z, n_y = lax.axis_size("z"), lax.axis_size("y")
    owners = lax.axis_size(DP)
    tensor_at = lax.axis_index(TENSOR)
    n_tensor = lax.axis_size(TENSOR)
    width = norm_gain.shape[0]
    quarter = width // n_tensor

    cols = out_proj.shape[1]
    depth = out_proj.shape[0] // n_z
    proj = out_proj.T.reshape(cols, n_z, depth).transpose(1, 0, 2)
    proj = exchange(proj, "z")
    values = attention(queries, latent_cache, lengths, value_up)
    proj, values = lax.optimization_barrier((proj, values))
    half = n_z // 2
    proj_leaving = lax.dynamic_slice_in_dim(proj, (1 - xl) * half, half, 0)
    proj_other = flip(proj_leaving, "xl")
    proj_mine = lax.dynamic_slice_in_dim(proj, xl * half, half, 0)
    over_y = jnp.concatenate([proj_mine, proj_other], axis=0)
    over_y = [over_y] + [flip(over_y, "y", s) for s in range(1, n_y)]
    values = values.reshape(rows_here, n_z, depth).transpose(1, 0, 2)
    values = exchange(values, "z").reshape(n_z * rows_here, depth)
    from_xh = flip(values, "xh")
    from_both = flip(values, ("xh", "xl"), 3)
    over_y[1], values_late = lax.optimization_barrier((over_y[1], values))
    from_xl = flip(values_late, "xl")
    over_y = jnp.stack(over_y)
    over_y = over_y.reshape(n_y, 2, half, cols, depth)
    over_y = jnp.stack(
        [lax.dynamic_index_in_dim(over_y, y ^ s, 0, keepdims=False) for s in range(n_y)], axis=2
    )
    proj_own = over_y[0].reshape(quarter, depth)
    proj_oth = over_y[1].reshape(quarter, depth)

    here = xh == core
    keep_own, send_own = pair(here, values, from_xh)
    keep_oth, send_oth = pair(here, from_xl, from_both)
    partial_send = (dot_t(send_own, proj_own) + dot_t(send_oth, proj_oth)).astype(bf16)
    partial_got = flip(partial_send, "core")
    partial = dot_t(keep_own, proj_own) + dot_t(keep_oth, proj_oth) + partial_got.astype(f32)
    partial = partial.astype(bf16).reshape(n_z, rows_here, quarter)
    w_down, partial, routes_late = lax.optimization_barrier((w_down, partial, routes))
    partial = exchange(partial, "z")
    swap = [(i, (i % 2) * 2 + i // 2) for i in range(4)]
    routes_sent = lax.ppermute(routes_late, ("xh", "core"), swap)

    down = []
    for s in range(n_tensor):
        piece = lax.dynamic_slice_in_dim(w_down[0], (tensor_at ^ s) * quarter, quarter, 1)
        down.append(flip(piece, TENSOR, s) if s else piece)

    part_rows = jnp.sum(partial.astype(f32), axis=0).astype(bf16)

    _, slots_sent = placing(routes_sent, expert_home, owners)
    outgoing = jnp.einsum(
        "roc,rd->ocd", slots_sent.astype(bf16), part_rows, preferred_element_type=f32
    ).astype(bf16)
    outgoing, w_gate, w_up = lax.optimization_barrier((outgoing, w_gate, w_up))
    incoming = exchange(outgoing, DP).reshape(2, -1, quarter)

    def folded(weight, side):
        weight = weight.reshape(2, 2, quarter, -1)
        gains = norm_gain.reshape(2, 2, quarter, 1)
        weight = lax.dynamic_index_in_dim(weight, side, 1, keepdims=False)
        gains = lax.dynamic_index_in_dim(gains, side, 1, keepdims=False)
        return (weight.astype(f32) * gains).astype(bf16)

    halves = [[folded(w, side) for w in (w_gate, w_up)] for side in (xl, 1 - xl)]
    halves, incoming = lax.optimization_barrier((halves, incoming))
    in_xl = flip(incoming, "xl")
    in_core = flip(incoming, "core")
    in_both = flip(in_xl, "core")

    def from_half(pieces, weights):
        squares, gate_out, up_out = 0.0, 0.0, 0.0
        for i in (0, 1):
            rows = pieces[i].astype(f32)
            squares += jnp.sum(rows * rows, axis=1, keepdims=True)
            gate_out += jnp.dot(pieces[i], weights[0][i], preferred_element_type=f32)
            up_out += jnp.dot(pieces[i], weights[1][i], preferred_element_type=f32)
        return squares, gate_out, up_out

    def hidden_of(own_half, other_half):
        squares, gate_out, up_out = (
            one + two
            for one, two in zip(from_half(own_half, halves[0]), from_half(other_half, halves[1]))
        )
        scale = lax.rsqrt(squares / width + norm_eps)
        return (jax.nn.silu(gate_out * scale) * (up_out * scale)).astype(bf16)

    hidden = jnp.concatenate(
        pair(core == 0, hidden_of(incoming, in_xl), hidden_of(in_core, in_both)), axis=0
    )
    hid_xl = flip(hidden, "xl")
    hid_core = flip(hidden, "core")
    result = jnp.dot(hidden, down[0], preferred_element_type=f32)
    result += jnp.dot(hid_core, down[1], preferred_element_type=f32)
    row_xl = flip(part_rows, "xl")
    lower, upper = pair(xl == 0, part_rows, row_xl)
    mine = jnp.concatenate([lower, upper], axis=1)
    row_xh = flip(mine, "xh")
    lower, upper = pair(xh == 0, mine, row_xh)
    whole = jnp.concatenate([lower, upper], axis=1)
    result, hid_xl, whole = lax.optimization_barrier((result, hid_xl, whole))
    hid_both = flip(hid_xl, "core")
    result += jnp.dot(hid_xl, down[2], preferred_element_type=f32)
    result += jnp.dot(hid_both, down[3], preferred_element_type=f32)
    returned = exchange(result.astype(bf16).reshape(owners, MOST, quarter), DP)

    on_owner, slot_map = placing(routes, expert_home, owners)
    share_weight = jnp.sum(jnp.where(on_owner, route_weight[:, :, None], 0.0), axis=1)
    combine_weight = slot_map.astype(f32) * share_weight[:, :, None]
    experts_out = jnp.einsum("roc,ocd->rd", combine_weight, returned.astype(f32)).astype(bf16)

    attended = jnp.where(here, whole, flip(whole, "core"))
    return (attended, experts_out)


def solution(mesh):
    fine = Mesh(mesh.devices.reshape(2, 8, 4, 2, 2), AXES)
    return jax.shard_map(
        shards,
        mesh=fine,
        in_specs=(
            P(DP, TENSOR, None),
            P(DP, None, None),
            P(DP),
            P(TENSOR, None, None),
            P(TENSOR, DP),
            P(),
            P(DP, None),
            P(DP, None),
            P(),
            P(DP, None, TENSOR),
            P(DP, None, TENSOR),
            P(DP, TENSOR, None),
        ),
        out_specs=(P(DP, None), P(DP, TENSOR)),
        check_vma=False,
    )
```

```python
import jax
import jax.numpy as jnp
from jax import lax
from jax.sharding import Mesh, PartitionSpec as P

LATENT = 512
MOST = 4

softmax_scale = 192.0 ** (-0.5)
norm_eps = 1e-06

AXES = ("xh", "z", "y", "xl", "core")
DP = ("xh", "z", "y")
TENSOR = ("xl", "core")
bf16 = jnp.bfloat16
f32 = jnp.float32


def flip(value, axis, mask=1):
    count = lax.axis_size(axis)
    return lax.ppermute(value, axis, [(i, i ^ mask) for i in range(count)])


def exchange(value, axis):
    return lax.all_to_all(value, axis, split_axis=0, concat_axis=0, tiled=True)


def dot_t(left, right):
    return lax.dot_general(left, right, (((1,), (1,)), ((), ())), preferred_element_type=f32)


def pair(where_zero, mine, other):
    return jnp.where(where_zero, mine, other), jnp.where(where_zero, other, mine)


def attention(queries, latent_cache, lengths, value_up):
    scores = (
        jnp.einsum("rhc,rjc->rhj", queries, latent_cache, preferred_element_type=f32)
        * softmax_scale
    )
    visible = (
        lax.broadcasted_iota(jnp.int32, (1, 1, latent_cache.shape[1]), 2) < lengths[:, None, None]
    )
    scores = jnp.where(visible, scores, -jnp.inf)
    row_max = jnp.max(scores, axis=2, keepdims=True)
    exponent = jnp.exp(scores - row_max)
    weights = (exponent / jnp.sum(exponent, axis=2, keepdims=True)).astype(bf16)
    latent_out = jnp.einsum(
        "rhj,rjc->rhc", weights, latent_cache[:, :, :LATENT], preferred_element_type=f32
    ).astype(bf16)
    values = jnp.einsum("rhc,hcv->rhv", latent_out, value_up, preferred_element_type=f32)
    return values.astype(bf16).reshape(queries.shape[0], -1)


def placing(routes, expert_home, owners):
    catalog = jnp.arange(expert_home.shape[0], dtype=jnp.int32)
    matches = routes[:, :, None] == catalog[None, None, :]
    home_of = jnp.sum(jnp.where(matches, expert_home[None, None, :], 0), axis=2)
    owner_ids = jnp.arange(owners, dtype=jnp.int32)
    on_owner = home_of[:, :, None] == owner_ids[None, None, :]
    chosen = jnp.any(on_owner, axis=1)
    order_in = jnp.cumsum(chosen.astype(jnp.int32), axis=0) - 1
    slot_ids = jnp.arange(MOST, dtype=jnp.int32)
    slot_map = chosen[:, :, None] & (order_in[:, :, None] == slot_ids[None, None, :])
    return on_owner, slot_map


def shards(
    queries,
    latent_cache,
    lengths,
    value_up,
    out_proj,
    norm_gain,
    routes,
    route_weight,
    expert_home,
    w_gate,
    w_up,
    w_down,
):
    rows_here = queries.shape[0]
    xh, y, xl, core = (lax.axis_index(name) for name in ("xh", "y", "xl", "core"))
    n_z, n_y = lax.axis_size("z"), lax.axis_size("y")
    owners = lax.axis_size(DP)
    tensor_at = lax.axis_index(TENSOR)
    n_tensor = lax.axis_size(TENSOR)
    width = norm_gain.shape[0]
    quarter = width // n_tensor

    cols = out_proj.shape[1]
    depth = out_proj.shape[0] // n_z
    proj = out_proj.T.reshape(cols, n_z, depth).transpose(1, 0, 2)
    proj = exchange(proj, "z")
    values = attention(queries, latent_cache, lengths, value_up)
    proj, values = lax.optimization_barrier((proj, values))
    half = n_z // 2
    proj_leaving = lax.dynamic_slice_in_dim(proj, (1 - xl) * half, half, 0)
    proj_other = flip(proj_leaving, "xl")
    proj_mine = lax.dynamic_slice_in_dim(proj, xl * half, half, 0)
    over_y = jnp.concatenate([proj_mine, proj_other], axis=0)
    over_y = [over_y] + [flip(over_y, "y", s) for s in range(1, n_y)]
    values = values.reshape(rows_here, n_z, depth).transpose(1, 0, 2)
    values = exchange(values, "z").reshape(n_z * rows_here, depth)
    from_xh = flip(values, "xh")
    from_both = flip(values, ("xh", "xl"), 3)
    over_y[1], values_late = lax.optimization_barrier((over_y[1], values))
    from_xl = flip(values_late, "xl")
    over_y = jnp.stack(over_y)
    over_y = over_y.reshape(n_y, 2, half, cols, depth)
    over_y = jnp.stack(
        [lax.dynamic_index_in_dim(over_y, y ^ s, 0, keepdims=False) for s in range(n_y)], axis=2
    )
    proj_own = over_y[0].reshape(quarter, depth)
    proj_oth = over_y[1].reshape(quarter, depth)

    here = xh == core
    keep_own, send_own = pair(here, values, from_xh)
    keep_oth, send_oth = pair(here, from_xl, from_both)
    partial_send = (dot_t(send_own, proj_own) + dot_t(send_oth, proj_oth)).astype(bf16)
    partial_got = flip(partial_send, "core")
    partial = dot_t(keep_own, proj_own) + dot_t(keep_oth, proj_oth) + partial_got.astype(f32)
    partial = partial.astype(bf16).reshape(n_z, rows_here, quarter)
    w_down, partial, routes_late = lax.optimization_barrier((w_down, partial, routes))
    partial = exchange(partial, "z")
    swap = [(i, (i % 2) * 2 + i // 2) for i in range(4)]
    routes_sent = lax.ppermute(routes_late, ("xh", "core"), swap)

    down = []
    for s in range(n_tensor):
        piece = lax.dynamic_slice_in_dim(w_down[0], (tensor_at ^ s) * quarter, quarter, 1)
        down.append(flip(piece, TENSOR, s) if s else piece)

    part_rows = jnp.sum(partial.astype(f32), axis=0).astype(bf16)

    _, slots_sent = placing(routes_sent, expert_home, owners)
    slots_sent = slots_sent.astype(bf16).reshape(rows_here, owners * MOST)
    outgoing = lax.dot_general(
        slots_sent, part_rows, (((0,), (0,)), ((), ())), preferred_element_type=f32
    ).astype(bf16)
    outgoing = outgoing.reshape(owners, MOST, quarter)
    outgoing, w_gate, w_up = lax.optimization_barrier((outgoing, w_gate, w_up))
    incoming = exchange(outgoing, DP).reshape(2, -1, quarter)

    def folded(weight, side):
        weight = weight.reshape(2, 2, quarter, -1)
        gains = norm_gain.reshape(2, 2, quarter, 1)
        weight = lax.dynamic_index_in_dim(weight, side, 1, keepdims=False)
        gains = lax.dynamic_index_in_dim(gains, side, 1, keepdims=False)
        return (weight.astype(f32) * gains).astype(bf16)

    halves = [[folded(w, side) for w in (w_gate, w_up)] for side in (xl, 1 - xl)]
    halves, incoming = lax.optimization_barrier((halves, incoming))
    in_xl = flip(incoming, "xl")
    in_core = flip(incoming, "core")
    in_both = flip(in_xl, "core")

    def from_half(pieces, weights):
        squares, gate_out, up_out = 0.0, 0.0, 0.0
        for i in (0, 1):
            rows = pieces[i].astype(f32)
            squares += jnp.sum(rows * rows, axis=1, keepdims=True)
            gate_out += jnp.dot(pieces[i], weights[0][i], preferred_element_type=f32)
            up_out += jnp.dot(pieces[i], weights[1][i], preferred_element_type=f32)
        return squares, gate_out, up_out

    def hidden_of(own_half, other_half):
        squares, gate_out, up_out = (
            one + two
            for one, two in zip(from_half(own_half, halves[0]), from_half(other_half, halves[1]))
        )
        scale = lax.rsqrt(squares / width + norm_eps)
        return (jax.nn.silu(gate_out * scale) * (up_out * scale)).astype(bf16)

    hidden = jnp.concatenate(
        pair(core == 0, hidden_of(incoming, in_xl), hidden_of(in_core, in_both)), axis=0
    )
    hid_xl = flip(hidden, "xl")
    hid_core = flip(hidden, "core")
    result = jnp.dot(hidden, down[0], preferred_element_type=f32)
    result += jnp.dot(hid_core, down[1], preferred_element_type=f32)
    row_xl = flip(part_rows, "xl")
    lower, upper = pair(xl == 0, part_rows, row_xl)
    mine = jnp.concatenate([lower, upper], axis=1)
    row_xh = flip(mine, "xh")
    lower, upper = pair(xh == 0, mine, row_xh)
    whole = jnp.concatenate([lower, upper], axis=1)
    result, hid_xl, whole = lax.optimization_barrier((result, hid_xl, whole))
    hid_both = flip(hid_xl, "core")
    result += jnp.dot(hid_xl, down[2], preferred_element_type=f32)
    result += jnp.dot(hid_both, down[3], preferred_element_type=f32)
    returned = exchange(result.astype(bf16).reshape(owners, MOST, quarter), DP)

    on_owner, slot_map = placing(routes, expert_home, owners)
    share_weight = jnp.sum(jnp.where(on_owner, route_weight[:, :, None], 0.0), axis=1)
    combine_weight = slot_map.astype(f32) * share_weight[:, :, None]
    experts_out = jnp.einsum("roc,ocd->rd", combine_weight, returned.astype(f32)).astype(bf16)

    attended = jnp.where(here, whole, flip(whole, "core"))
    return (attended, experts_out)


def solution(mesh):
    fine = Mesh(mesh.devices.reshape(2, 8, 4, 2, 2), AXES)
    return jax.shard_map(
        shards,
        mesh=fine,
        in_specs=(
            P(DP, TENSOR, None),
            P(DP, None, None),
            P(DP),
            P(TENSOR, None, None),
            P(TENSOR, DP),
            P(),
            P(DP, None),
            P(DP, None),
            P(),
            P(DP, None, TENSOR),
            P(DP, None, TENSOR),
            P(DP, TENSOR, None),
        ),
        out_specs=(P(DP, None), P(DP, TENSOR)),
        check_vma=False,
    )
```
